32 devices in a mesh: lat: 4 (over z), lon: 4 (over y, x), ens: 2 (over core).
Axes of the slice: x: 2, y: 2, z: 4, core: 2. Of those that a mesh axis runs over, the one named last changes fastest.
Arguments:
- band_field: bfloat16 [256, 256, 360], P(('ens', 'lat'), 'lon'), parts along dimension 0, may hold values from -6 to 6
- offsets: int32 [128, 4], P('lat'), may hold values from -3 to 3, as said below
- live_counts: int32 [128], P('lat'), may hold values from 1 to 4, as said below
- band_ids: int32 [128, 4], P('lat'), may hold values from 0 to 7
- tap_bank: bfloat16 [9, 8, 128], replicated, as said below
- mixing: bfloat16 [9, 64, 256], replicated, may hold values from -0.25 to 0.25
Outputs:
- convolved: bfloat16 [256, 360, 256], P(('ens', 'lat'), 'lon'), parts along dimension 0
The draws below stay inside these ranges and needn't reach their ends.
There are 2 independent parts, one for each index of `ens`. The reference program is written for one: setup_inputs(seed, part) draws one part's arguments, and reference() takes and returns one part's arrays. A program takes and returns all parts, laid end to end along the dimension named above; an argument that names none is the same for every part. Nothing has to cross between parts.
Inputs may be any that keep to these rules, and one draw needn't show every extreme that they name: Row i + offsets[i, s] lies in the grid of 128 rows; offsets[i, 0] is 0; offsets of -3 and +3 both occur. Slots s >= live_counts[i] of row i are unused. tap_bank[k, b, d] is zero unless -r <= d - 64 < r, with r = (64 * (b + 1)) // 8.
All inputs are finite; a program needn't handle non-finite values.
Results may differ from the reference program's by a relative error of at most 0.0049.
Values may be sent and summed in bfloat16 or wider, within the bound.
A program may use at most 128 MiB of HBM per device.

```python
import jax
import jax.numpy as jnp
import numpy as np
from jax import lax

CHANNELS = 256
GROUPS = 4
BASIS = 9
REACH = 64
HALO = 3
BANDS = 8
SLOTS = 4
NLAT = 128
NLON = 360


def draw_offsets(key, part):
    key = jax.random.fold_in(key, 11)
    row_ids = jnp.arange(NLAT, dtype=jnp.int32)[:, None]
    slot_ids = jnp.arange(SLOTS, dtype=jnp.int32)[None, :]
    drawn = jax.random.randint(key, (NLAT, SLOTS), -HALO, HALO + 1, dtype=jnp.int32)
    drawn = jnp.clip(drawn, -row_ids, NLAT - 1 - row_ids)
    drawn = jnp.where(slot_ids == 0, 0, drawn)
    drawn = jnp.where((row_ids == HALO) & (slot_ids == 1), -HALO, drawn)
    drawn = jnp.where((row_ids == NLAT - 1 - HALO) & (slot_ids == 1), HALO, drawn)
    return drawn.astype(jnp.int32)


def draw_live_counts(key, part):
    key = jax.random.fold_in(key, 23)
    row_ids = jnp.arange(NLAT, dtype=jnp.int32)
    polar_level = jnp.abs(2 * row_ids + 1 - NLAT) * (SLOTS - 1) // (NLAT - 1)
    extra = jax.random.randint(key, (NLAT,), 1, 3, dtype=jnp.int32)
    return jnp.clip(polar_level + extra, 1, SLOTS).astype(jnp.int32)


def draw_band_ids(key, part):
    key = jax.random.fold_in(key, 37)
    row_ids = jnp.arange(NLAT, dtype=jnp.int32)[:, None]
    slot_ids = jnp.arange(SLOTS, dtype=jnp.int32)[None, :]
    polar_level = jnp.abs(2 * row_ids + 1 - NLAT) * (BANDS - 1) // (NLAT - 1)
    lowered = jax.random.randint(key, (NLAT, SLOTS), 0, 2, dtype=jnp.int32)
    lowered = jnp.where(slot_ids == 0, 0, lowered)
    return jnp.clip(polar_level - lowered, 0, BANDS - 1).astype(jnp.int32)


def draw_tap_bank(key, part):
    key = jax.random.fold_in(key, 41)
    band_axis = jnp.arange(BANDS, dtype=jnp.int32)[None, :, None]
    tap_axis = jnp.arange(2 * REACH, dtype=jnp.int32)[None, None, :] - REACH
    reach_cells = REACH * (band_axis + 1) // BANDS
    inside = (tap_axis >= -reach_cells) & (tap_axis < reach_cells)
    tap_scale = 1.0 / jnp.sqrt(2.0 * reach_cells.astype(jnp.float32) * SLOTS)
    drawn = jax.random.normal(key, (BASIS, BANDS, 2 * REACH), jnp.float32)
    return jnp.where(inside, drawn * tap_scale, 0.0).astype(jnp.bfloat16)


def steps_of(stream_key, extent, split, smallest, top_value):
    loudness = 1.0
    for dim, parts in split:
        heights = jax.random.uniform(jax.random.fold_in(jax.random.fold_in(stream_key, 6), dim), (parts,), jnp.float32, smallest / len(split), top_value / len(split))
        loudness = loudness * jnp.repeat(jnp.exp(heights), extent[dim] // parts).reshape((-1,) + (1,) * (len(extent) - 1 - dim))
    return loudness


def normal_values(key, shape, scale, reach, shards=(), kind=jnp.bfloat16):
    array = jax.random.normal(key, shape, jnp.float32) * scale
    if len(shards) > 0:
        array = steps_of(key, shape, shards, -0.22, 0.18) * array
    return jnp.clip(array, min=-reach, max=reach).astype(kind)


def setup_inputs(seed: int = 0, part: int = 0) -> dict:
    splits = jax.random.split(jax.random.key(seed), 7)
    own_keys = jax.random.split(jax.random.fold_in(splits[6], part), 7)
    band_field = normal_values(own_keys[0], (NLAT, CHANNELS, NLON), 1.0, 6.0, ((0, 4), (1, 4)))
    offsets = draw_offsets(jax.random.fold_in(splits[6], 71), part)
    live_counts = draw_live_counts(jax.random.fold_in(splits[6], 71), part)
    band_ids = draw_band_ids(jax.random.fold_in(splits[6], 71), part)
    tap_bank = draw_tap_bank(jax.random.fold_in(splits[6], 71), part)
    mixing = normal_values(splits[5], (BASIS, CHANNELS // GROUPS, CHANNELS), (BASIS * CHANNELS // GROUPS) ** -0.5, 0.25)
    return {"band_field": band_field, "offsets": offsets, "live_counts": live_counts, "band_ids": band_ids, "tap_bank": tap_bank, "mixing": mixing}


def reference(band_field, offsets, live_counts, band_ids, tap_bank, mixing):
    field_wide = band_field.astype(jnp.float32)
    spectra = jnp.fft.rfft(field_wide, axis=2)
    position = (REACH - np.arange(2 * REACH)) % NLON
    kernels = jnp.zeros((BASIS, BANDS, NLON), jnp.float32).at[:, :, position].set(tap_bank.astype(jnp.float32))
    responses = jnp.fft.rfft(kernels, axis=2)
    group_width = CHANNELS // GROUPS
    mixing_wide = mixing.astype(jnp.float32).reshape(BASIS, group_width, GROUPS, group_width)

    def one_row(packed):
        row_index, offset_row, live_count, band_row = packed
        summed = jnp.zeros((BASIS, CHANNELS, NLON // 2 + 1), responses.dtype)
        for slot_index in range(SLOTS):
            source = lax.dynamic_index_in_dim(spectra, (row_index + offset_row[slot_index]).astype(jnp.int32), 0, keepdims=False)
            response = lax.dynamic_index_in_dim(responses, band_row[slot_index].astype(jnp.int32), 1, keepdims=False)
            live_mask = (slot_index < live_count).astype(jnp.float32)
            summed = summed + live_mask * response[:, None, :] * source[None]
        quadrature = jnp.fft.irfft(summed, n=NLON, axis=2).astype(jnp.float32).astype(jnp.bfloat16)
        quadrature = lax.optimization_barrier(quadrature)
        grouped = quadrature.astype(jnp.float32).reshape(BASIS, GROUPS, group_width, NLON)
        mixed_rows = jnp.einsum("kcgo,kgcl->lgo", mixing_wide, grouped)
        return mixed_rows.reshape(NLON, CHANNELS).astype(jnp.bfloat16)

    row_ids = jnp.arange(NLAT, dtype=jnp.int32)
    return lax.map(one_row, (row_ids, offsets, live_counts, band_ids))
```

```python
import functools

import jax
import jax.numpy as jnp
from jax import lax
from jax.experimental import pallas as pl
from jax.experimental.pallas import tpu as pltpu
from jax.sharding import PartitionSpec as P

GROUPS = 4
BASIS = 9
REACH = 64
HALO = 3
SLOTS = 4


def extended_2(x, sides, width, wrap):
    for axis, dim in sides:
        size, length = (lax.axis_size(axis), x.shape[dim])
        up = [(i, (i + 1) % size) for i in range(size if wrap else size - 1)]
        down = [(j, i) for i, j in up]
        last = lax.slice_in_dim(x, length - width, length, axis=dim)
        first = lax.slice_in_dim(x, 0, width, axis=dim)
        before = lax.ppermute(last, axis, up)
        after = lax.ppermute(first, axis, down)
        x = jnp.concatenate([before, x, after], axis=dim)
    return x


def tiled_plan(band_field, offsets, live_counts, band_ids, tap_bank, mixing):
    tiles = lax.all_to_all(band_field, "lon", split_axis=2, concat_axis=1, tiled=True)
    widened = extended_2(tiles, (("lon", 2),), REACH, True)
    extended = extended_2(widened, (("lat", 0),), HALO, False)
    channels = extended.shape[1]
    span_cells = extended.shape[2]
    lon_cells = span_cells - 2 * REACH
    group_width = channels // GROUPS
    mixing_split = mixing.reshape(BASIS, group_width, GROUPS, group_width)
    distance = lax.broadcasted_iota(jnp.int32, (span_cells, lon_cells), 0) - lax.broadcasted_iota(
        jnp.int32, (span_cells, lon_cells), 1
    )
    inside = (distance >= 0) & (distance < 2 * REACH)
    picked = jnp.take(tap_bank, jnp.clip(distance, 0, 2 * REACH - 1), axis=2)
    toeplitz = jnp.where(inside, picked, jnp.zeros((), tap_bank.dtype))

    def slot_term(row_index, offset, band_index):
        source = lax.dynamic_index_in_dim(extended, row_index + HALO + offset, 0, keepdims=False)
        matrix = lax.dynamic_index_in_dim(toeplitz, band_index, 1, keepdims=False)
        return jnp.einsum("cj,kjl->kcl", source, matrix, preferred_element_type=jnp.float32)

    def one_row(packed):
        row_index, offset_row, live_count, band_row = packed
        summed = jnp.zeros((BASIS, channels, lon_cells), jnp.float32)
        for slot_index in range(SLOTS):
            live_mask = (slot_index < live_count).astype(jnp.float32)
            summed = summed + live_mask * slot_term(
                row_index, offset_row[slot_index], band_row[slot_index]
            )
        quadrature = summed.astype(jnp.bfloat16).reshape(BASIS, GROUPS, group_width, lon_cells)
        mixed_rows = jnp.einsum(
            "kcgo,kgcl->lgo", mixing_split, quadrature, preferred_element_type=jnp.float32
        )
        return mixed_rows.reshape(lon_cells, channels).astype(jnp.bfloat16)

    local_rows = jnp.arange(offsets.shape[0], dtype=jnp.int32)
    return lax.map(one_row, (local_rows, offsets, live_counts, band_ids))


NT=(((1,),(1,)),((),()))
def kernel(R, mode, off_ref, live_ref, band_ref, xp_ref, taps_ref, m4_ref, out_ref, T_ref, W_ref, bd_ref, q_ref):
    step = pl.program_id(0)
    def window(r):
        for t in range(4):
            W_ref[r, t*64:(t+1)*64, :] = xp_ref[r, :, 90*t:90*t+256] if t < 3 else jnp.concatenate([xp_ref[r, :, 270:512], xp_ref[r,:,0:14]], axis=1)
    @pl.when(step == 0)
    def _():
        def build(i, c):
            row = jnp.broadcast_to(taps_ref[pl.ds(i, 1), :], (96, 256))
            T_ref[i] = pltpu.roll(row, 0, 1, stride=1, stride_axis=0).astype(jnp.bfloat16)
            return c
        lax.fori_loop(0, 72, build, 0, unroll=4)
        lane = lax.broadcasted_iota(jnp.int32, (64, 256), 1) // 64
        for t in range(4):
            for k in range(9):
                bd_ref[k, t*64:(t+1)*64, :] = jnp.where(lane == t, m4_ref[k], jnp.zeros((), jnp.bfloat16))
        def wb(r, c):
            window(r); return c
        lax.fori_loop(0, 38, wb, 0)
    for r in range(R):
        i = step * R + r
        def slots(n):
            acc = None
            for s in range(n):
                tb = T_ref[pl.ds(band_ref[i*4+s] * 9, 9)].reshape(864, 256)
                if mode == 0:
                    tb = jnp.where(s < live_ref[i], tb, jnp.zeros_like(tb))
                d = lax.dot_general(tb, W_ref[i + 3 + off_ref[i*4+s]], NT, preferred_element_type=jnp.float32)
                acc = d if acc is None else acc + d
            q_ref[:, r*96:(r+1)*96, :] = acc.astype(jnp.bfloat16).reshape(9, 96, 256)
        if mode == 0 or mode == 2:
            slots(4)
        else:
            for n in range(1, 5):
                pl.when(live_ref[i] == n)(functools.partial(slots, n))
    acc = None
    for k in range(9):
        d = jnp.dot(q_ref[k], bd_ref[k], preferred_element_type=jnp.float32)
        acc = d if acc is None else acc + d
    low = lax.broadcasted_iota(jnp.int32, (96, 128), 1) < 64
    for p in range(R//2):
        a0 = acc[p*192:p*192+96]; a1 = acc[p*192+96:p*192+192]
        for h in range(2):
            b0 = a0[:, h*128:(h+1)*128]; b1 = a1[:, h*128:(h+1)*128]
            out_ref[2*h, p] = jnp.where(low, b0, pltpu.roll(b1, 64, 1)).astype(jnp.bfloat16)
            out_ref[2*h+1, p] = jnp.where(low, pltpu.roll(b0, 64, 1), b1).astype(jnp.bfloat16)

def conv(off, live, band, xp, taps, m4, R=4, mode=1):
    rows = live.shape[0]
    sm = pl.BlockSpec(memory_space=pltpu.SMEM); vm = pl.BlockSpec(memory_space=pltpu.VMEM)
    return pl.pallas_call(functools.partial(kernel, R, mode), grid=(rows//R,),
        out_shape=jax.ShapeDtypeStruct((4, rows//2, 96, 128), jnp.bfloat16),
        in_specs=[sm,sm,sm,vm,vm,vm],
        out_specs=pl.BlockSpec((4, R//2, 96, 128), lambda s: (0, s, 0, 0)),
        scratch_shapes=[pltpu.VMEM((72,96,256), jnp.bfloat16), pltpu.VMEM((rows+6,256,256), jnp.bfloat16),
          pltpu.VMEM((9,256,256), jnp.bfloat16), pltpu.VMEM((9,R*96,256), jnp.bfloat16)],
        compiler_params=pltpu.CompilerParams(vmem_limit_bytes=48*2**20),
    )(off.reshape(-1), live, band.reshape(-1), xp, taps, m4)

def grouped_plan(band_field, offsets, live_counts, band_ids, tap_bank, mixing):
    rows = band_field.shape[0]
    size = lax.axis_size("lat")
    up = [(i, i + 1) for i in range(size - 1)]
    before = lax.ppermute(band_field[rows - HALO:], "lat", up)
    after = lax.ppermute(band_field[:HALO], "lat", [(j, i) for i, j in up])
    x = jnp.concatenate([before, band_field, after], axis=0)
    xp = jnp.concatenate([x[..., 360 - REACH:], x, x[..., :88]], axis=-1)
    tp = jnp.pad(tap_bank.transpose(1, 0, 2).astype(jnp.float32), ((0, 0), (0, 0), (0, 128))).reshape(72, 256)
    group = lax.axis_index("lon")
    own = lax.dynamic_slice_in_dim(mixing, group * 64, 64, axis=2)
    out = conv(offsets, live_counts, band_ids, xp, tp, jnp.tile(own, (1, 1, 4)))
    got = lax.all_to_all(out, "lon", split_axis=0, concat_axis=0, tiled=True)
    got = got[:, :, :90].reshape(4, rows // 2, 90, 2, 64)
    return got.transpose(1, 3, 2, 0, 4).reshape(rows, 90, 256)


def solution(mesh):
    def on_device(*args):
        field = args[0]
        if field.shape[1] == 256 // GROUPS and field.shape[2] == 360 and mesh.shape["lon"] == 4 and field.shape[0] % 4 == 0:
            return grouped_plan(*args)
        return tiled_plan(*args)

    placed = (P(("ens", "lat"), "lon", None), P("lat", None), P("lat"), P("lat", None), P(), P())
    return jax.shard_map(
        on_device,
        mesh=mesh,
        in_specs=placed,
        out_specs=P(("ens", "lat"), "lon", None),
        check_vma=False,
    )
```

```python
import jax
import jax.numpy as jnp
from jax import lax
from jax.experimental import pallas as pl
from jax.experimental.pallas import tpu as pltpu
from jax.sharding import PartitionSpec as P

GROUPS = 4
BASIS = 9
REACH = 64
HALO = 3
SLOTS = 4


def extended_2(x, sides, width, wrap):
    for axis, dim in sides:
        size, length = (lax.axis_size(axis), x.shape[dim])
        up = [(i, (i + 1) % size) for i in range(size if wrap else size - 1)]
        down = [(j, i) for i, j in up]
        last = lax.slice_in_dim(x, length - width, length, axis=dim)
        first = lax.slice_in_dim(x, 0, width, axis=dim)
        before = lax.ppermute(last, axis, up)
        after = lax.ppermute(first, axis, down)
        x = jnp.concatenate([before, x, after], axis=dim)
    return x


def tiled_plan(band_field, offsets, live_counts, band_ids, tap_bank, mixing):
    tiles = lax.all_to_all(band_field, "lon", split_axis=2, concat_axis=1, tiled=True)
    widened = extended_2(tiles, (("lon", 2),), REACH, True)
    extended = extended_2(widened, (("lat", 0),), HALO, False)
    channels = extended.shape[1]
    span_cells = extended.shape[2]
    lon_cells = span_cells - 2 * REACH
    group_width = channels // GROUPS
    mixing_split = mixing.reshape(BASIS, group_width, GROUPS, group_width)
    distance = lax.broadcasted_iota(jnp.int32, (span_cells, lon_cells), 0) - lax.broadcasted_iota(
        jnp.int32, (span_cells, lon_cells), 1
    )
    inside = (distance >= 0) & (distance < 2 * REACH)
    picked = jnp.take(tap_bank, jnp.clip(distance, 0, 2 * REACH - 1), axis=2)
    toeplitz = jnp.where(inside, picked, jnp.zeros((), tap_bank.dtype))

    def slot_term(row_index, offset, band_index):
        source = lax.dynamic_index_in_dim(extended, row_index + HALO + offset, 0, keepdims=False)
        matrix = lax.dynamic_index_in_dim(toeplitz, band_index, 1, keepdims=False)
        return jnp.einsum("cj,kjl->kcl", source, matrix, preferred_element_type=jnp.float32)

    def one_row(packed):
        row_index, offset_row, live_count, band_row = packed
        summed = jnp.zeros((BASIS, channels, lon_cells), jnp.float32)
        for slot_index in range(SLOTS):
            live_mask = (slot_index < live_count).astype(jnp.float32)
            summed = summed + live_mask * slot_term(
                row_index, offset_row[slot_index], band_row[slot_index]
            )
        quadrature = summed.astype(jnp.bfloat16).reshape(BASIS, GROUPS, group_width, lon_cells)
        mixed_rows = jnp.einsum(
            "kcgo,kgcl->lgo", mixing_split, quadrature, preferred_element_type=jnp.float32
        )
        return mixed_rows.reshape(lon_cells, channels).astype(jnp.bfloat16)

    local_rows = jnp.arange(offsets.shape[0], dtype=jnp.int32)
    return lax.map(one_row, (local_rows, offsets, live_counts, band_ids))


NT = (((1,), (1,)), ((), ()))
STEP = 4
TILE = 90
SPAN = 256
LINES = 96


def kernel(off_ref, live_ref, band_ref, x_ref, taps_ref, mix_ref, out_ref, bank, field, halo, weights, quad, send, recv, send_sem, recv_sem, halo_send, halo_recv):
    me = lax.axis_index("lon")
    lat = lax.axis_index("lat")
    n_lat = lax.axis_size("lat")
    rows = x_ref.shape[0]
    steps = rows // STEP
    above, below = lax.rem(lat + 1, n_lat), lax.rem(lat + n_lat - 1, n_lat)
    partners = [lax.rem(me + d, 4) for d in range(1, 4)]
    sources = [lax.rem(me + 4 - d, 4) for d in range(1, 4)]

    barrier = pltpu.get_barrier_semaphore()
    for p in partners:
        pl.semaphore_signal(barrier, inc=1, device_id={"lon": p}, device_id_type=pl.DeviceIdType.MESH)
    for q in (above, below):
        pl.semaphore_signal(barrier, inc=1, device_id={"lat": q}, device_id_type=pl.DeviceIdType.MESH)

    def window(x, slot):
        for t in range(4):
            s = (TILE * t - REACH) % 360
            if s + SPAN > 360:
                piece = jnp.concatenate([x[:, s:], x[:, : SPAN - 360 + s]], axis=1)
            else:
                piece = x[:, s : s + SPAN]
            field[slot, t * 64 : (t + 1) * 64, :] = piece

    def bank_block(i, c):
        line = jnp.broadcast_to(taps_ref[pl.ds(i, 1), :], (LINES, SPAN))
        bank[i] = pltpu.roll(line, 0, 1, stride=1, stride_axis=0).astype(jnp.bfloat16)
        return c

    lax.fori_loop(0, 72, bank_block, 0, unroll=4)
    bank[72:81] = jnp.zeros((9, LINES, SPAN), jnp.bfloat16)
    lane = lax.broadcasted_iota(jnp.int32, (64, SPAN), 1) // 64
    for t in range(4):
        for k in range(BASIS):
            weights[k * SPAN + t * 64 : k * SPAN + (t + 1) * 64, :] = jnp.where(lane == t, mix_ref[k], jnp.zeros((), jnp.bfloat16))

    def own_window(r, c):
        window(x_ref[r], r + HALO)
        return c

    lax.fori_loop(0, rows, own_window, 0)
    pl.semaphore_wait(barrier, 5)

    def halo_copy(n):
        return pltpu.make_async_remote_copy(
            src_ref=x_ref.at[pl.ds(rows - HALO if n == 0 else 0, HALO)],
            dst_ref=halo.at[n],
            send_sem=halo_send.at[n],
            recv_sem=halo_recv.at[n],
            device_id={"lat": above if n == 0 else below},
            device_id_type=pl.DeviceIdType.MESH,
        )

    for n in range(2):
        halo_copy(n).start()

    def chunk_copy(step, d):
        return pltpu.make_async_remote_copy(
            src_ref=send.at[partners[d], pl.ds(step * 2, 2)],
            dst_ref=recv.at[me, pl.ds(step * 2, 2)],
            send_sem=send_sem.at[d, step],
            recv_sem=recv_sem.at[d, step],
            device_id={"lon": partners[d]},
            device_id_type=pl.DeviceIdType.MESH,
        )

    low = lax.broadcasted_iota(jnp.int32, (LINES, 128), 1) < 64

    def body(idx, c):
        step = lax.rem(idx + 1, steps)

        @pl.when(idx == steps - 2)
        def _():
            for n in range(2):
                halo_copy(n).wait()
                for r in range(HALO):
                    window(halo[n, r], r + n * (rows + HALO))

        for r in range(STEP):
            i = step * STEP + r
            for k0 in range(0, BASIS, 3):
                acc = None
                for s in range(SLOTS):
                    b = jnp.where(s < live_ref[i], band_ref[i, s], 8)
                    part = lax.dot_general(
                        bank[pl.ds(b * BASIS + k0, 3)].reshape(3 * LINES, SPAN),
                        field[i + HALO + off_ref[i, s]],
                        NT,
                        preferred_element_type=jnp.float32,
                    )
                    acc = part if acc is None else acc + part
                for k in range(3):
                    quad[r * LINES : (r + 1) * LINES, (k0 + k) * SPAN : (k0 + k + 1) * SPAN] = acc[k * LINES : (k + 1) * LINES].astype(jnp.bfloat16)
        mixed = jnp.dot(quad[...], weights[...], preferred_element_type=jnp.float32)
        for p in range(STEP // 2):
            even = mixed[2 * p * LINES : (2 * p + 1) * LINES]
            odd = mixed[(2 * p + 1) * LINES : (2 * p + 2) * LINES]
            for h in range(2):
                e = even[:, h * 128 : (h + 1) * 128]
                o = odd[:, h * 128 : (h + 1) * 128]
                send[2 * h, step * 2 + p] = jnp.where(low, e, pltpu.roll(o, 64, 1)).astype(jnp.bfloat16)
                send[2 * h + 1, step * 2 + p] = jnp.where(low, pltpu.roll(e, 64, 1), o).astype(jnp.bfloat16)
        for d in range(3):
            chunk_copy(step, d).start()
        return c

    lax.fori_loop(0, steps, body, 0)

    def assemble(idx, c):
        step = lax.rem(idx + 1, steps)
        for d in range(3):
            chunk_copy(step, d).wait()
        recv[me, pl.ds(step * 2, 2)] = send[me, pl.ds(step * 2, 2)]
        for p in range(STEP // 2):
            pair = step * 2 + p
            for h in range(2):
                a = recv[2 * h, pair].astype(jnp.float32)
                b = recv[2 * h + 1, pair].astype(jnp.float32)
                out_ref[2 * pair, :, h * 128 : (h + 1) * 128] = jnp.where(low, a, pltpu.roll(b, 64, 1)).astype(jnp.bfloat16)[:TILE]
                out_ref[2 * pair + 1, :, h * 128 : (h + 1) * 128] = jnp.where(low, pltpu.roll(a, 64, 1), b).astype(jnp.bfloat16)[:TILE]
        return c

    lax.fori_loop(0, steps, assemble, 0)


def grouped_plan(band_field, offsets, live_counts, band_ids, tap_bank, mixing):
    rows = band_field.shape[0]
    steps = rows // STEP
    taps = jnp.pad(tap_bank.transpose(1, 0, 2).astype(jnp.float32), ((0, 0), (0, 0), (0, 128))).reshape(72, SPAN)
    own = jnp.tile(lax.dynamic_slice_in_dim(mixing, lax.axis_index("lon") * 64, 64, axis=2), (1, 1, 4))
    sm = pl.BlockSpec(memory_space=pltpu.SMEM)
    vm = pl.BlockSpec(memory_space=pltpu.VMEM)
    return pl.pallas_call(
        kernel,
        out_shape=jax.ShapeDtypeStruct((rows, TILE, 256), jnp.bfloat16),
        in_specs=[sm, sm, sm, vm, vm, vm],
        out_specs=vm,
        scratch_shapes=[
            pltpu.VMEM((81, LINES, SPAN), jnp.bfloat16),
            pltpu.VMEM((rows + 2 * HALO, SPAN, SPAN), jnp.bfloat16),
            pltpu.VMEM((2, HALO, 64, 360), jnp.bfloat16),
            pltpu.VMEM((BASIS * SPAN, SPAN), jnp.bfloat16),
            pltpu.VMEM((STEP * LINES, BASIS * SPAN), jnp.bfloat16),
            pltpu.VMEM((4, rows // 2, LINES, 128), jnp.bfloat16),
            pltpu.VMEM((4, rows // 2, LINES, 128), jnp.bfloat16),
            pltpu.SemaphoreType.DMA((3, steps)),
            pltpu.SemaphoreType.DMA((3, steps)),
            pltpu.SemaphoreType.DMA((2,)),
            pltpu.SemaphoreType.DMA((2,)),
        ],
        compiler_params=pltpu.CompilerParams(vmem_limit_bytes=48 * 2**20, collective_id=0, has_side_effects=True),
    )(offsets, live_counts, band_ids, band_field, taps, own)


def solution(mesh):
    def on_device(*args):
        field = args[0]
        grouped = field.shape[1] == 64 and field.shape[2] == 4 * TILE and mesh.shape["lon"] == 4 and mesh.shape["lat"] > 1
        if grouped and field.shape[0] % STEP == 0 and field.shape[0] >= 4 * STEP:
            return grouped_plan(*args)
        return tiled_plan(*args)

    placed = (P(("ens", "lat"), "lon", None), P("lat", None), P("lat"), P("lat", None), P(), P())
    return jax.shard_map(
        on_device,
        mesh=mesh,
        in_specs=placed,
        out_specs=P(("ens", "lat"), "lon", None),
        check_vma=False,
    )
```

```python
import jax
import jax.numpy as jnp
from jax import lax
from jax.experimental import pallas as pl
from jax.experimental.pallas import tpu as pltpu
from jax.sharding import PartitionSpec as P

GROUPS = 4
BASIS = 9
REACH = 64
HALO = 3
SLOTS = 4


def extended_2(x, sides, width, wrap):
    for axis, dim in sides:
        size, length = (lax.axis_size(axis), x.shape[dim])
        up = [(i, (i + 1) % size) for i in range(size if wrap else size - 1)]
        down = [(j, i) for i, j in up]
        last = lax.slice_in_dim(x, length - width, length, axis=dim)
        first = lax.slice_in_dim(x, 0, width, axis=dim)
        before = lax.ppermute(last, axis, up)
        after = lax.ppermute(first, axis, down)
        x = jnp.concatenate([before, x, after], axis=dim)
    return x


def tiled_plan(band_field, offsets, live_counts, band_ids, tap_bank, mixing):
    tiles = lax.all_to_all(band_field, "lon", split_axis=2, concat_axis=1, tiled=True)
    widened = extended_2(tiles, (("lon", 2),), REACH, True)
    extended = extended_2(widened, (("lat", 0),), HALO, False)
    channels = extended.shape[1]
    span_cells = extended.shape[2]
    lon_cells = span_cells - 2 * REACH
    group_width = channels // GROUPS
    mixing_split = mixing.reshape(BASIS, group_width, GROUPS, group_width)
    distance = lax.broadcasted_iota(jnp.int32, (span_cells, lon_cells), 0) - lax.broadcasted_iota(
        jnp.int32, (span_cells, lon_cells), 1
    )
    inside = (distance >= 0) & (distance < 2 * REACH)
    picked = jnp.take(tap_bank, jnp.clip(distance, 0, 2 * REACH - 1), axis=2)
    toeplitz = jnp.where(inside, picked, jnp.zeros((), tap_bank.dtype))

    def slot_term(row_index, offset, band_index):
        source = lax.dynamic_index_in_dim(extended, row_index + HALO + offset, 0, keepdims=False)
        matrix = lax.dynamic_index_in_dim(toeplitz, band_index, 1, keepdims=False)
        return jnp.einsum("cj,kjl->kcl", source, matrix, preferred_element_type=jnp.float32)

    def one_row(packed):
        row_index, offset_row, live_count, band_row = packed
        summed = jnp.zeros((BASIS, channels, lon_cells), jnp.float32)
        for slot_index in range(SLOTS):
            live_mask = (slot_index < live_count).astype(jnp.float32)
            summed = summed + live_mask * slot_term(
                row_index, offset_row[slot_index], band_row[slot_index]
            )
        quadrature = summed.astype(jnp.bfloat16).reshape(BASIS, GROUPS, group_width, lon_cells)
        mixed_rows = jnp.einsum(
            "kcgo,kgcl->lgo", mixing_split, quadrature, preferred_element_type=jnp.float32
        )
        return mixed_rows.reshape(lon_cells, channels).astype(jnp.bfloat16)

    local_rows = jnp.arange(offsets.shape[0], dtype=jnp.int32)
    return lax.map(one_row, (local_rows, offsets, live_counts, band_ids))


NT = (((1,), (1,)), ((), ()))
STEP = 4
TILE = 90
SPAN = 256
LINES = 96


def kernel(off_ref, live_ref, band_ref, x_ref, taps_ref, mix_ref, out_ref, bank, field, halo, weights, quad, send, recv, send_sem, recv_sem, halo_send, halo_recv):
    me = lax.axis_index("lon")
    lat = lax.axis_index("lat")
    n_lat = lax.axis_size("lat")
    rows = x_ref.shape[0]
    steps = rows // STEP
    above, below = lax.rem(lat + 1, n_lat), lax.rem(lat + n_lat - 1, n_lat)
    partners = [lax.rem(me + d, 4) for d in range(1, 4)]
    sources = [lax.rem(me + 4 - d, 4) for d in range(1, 4)]

    barrier = pltpu.get_barrier_semaphore()
    for p in partners:
        pl.semaphore_signal(barrier, inc=1, device_id={"lon": p}, device_id_type=pl.DeviceIdType.MESH)
    for q in (above, below):
        pl.semaphore_signal(barrier, inc=1, device_id={"lat": q}, device_id_type=pl.DeviceIdType.MESH)

    def window(x, slot):
        for t in range(4):
            s = (TILE * t - REACH) % 360
            if s + SPAN > 360:
                piece = jnp.concatenate([x[:, s:], x[:, : SPAN - 360 + s]], axis=1)
            else:
                piece = x[:, s : s + SPAN]
            field[slot, t * 64 : (t + 1) * 64, :] = piece

    def bank_blocks(k, c):
        taps = taps_ref[k].astype(jnp.float32)
        taps = jnp.concatenate([taps, jnp.zeros_like(taps)], axis=1)
        for b in range(8):
            line = jnp.broadcast_to(taps[b : b + 1], (16, SPAN))
            base = pltpu.roll(line, 0, 1, stride=1, stride_axis=0).astype(jnp.bfloat16)
            bank[b * BASIS + k, 0:16] = base
            for j in range(1, LINES // 16):
                bank[b * BASIS + k, 16 * j : 16 * (j + 1)] = jnp.concatenate([base[:, SPAN - 16 * j :], base[:, : SPAN - 16 * j]], axis=1)
        return c

    lax.fori_loop(0, BASIS, bank_blocks, 0)
    bank[72:81] = jnp.zeros((9, LINES, SPAN), jnp.bfloat16)
    half = lax.broadcasted_iota(jnp.int32, (64, 128), 1) < 64
    nothing = jnp.zeros((64, 128), jnp.float32)
    for k in range(BASIS):
        mix = mix_ref[k].astype(jnp.float32)
        near = jnp.where(me < 2, mix[:, :128], mix[:, 128:])
        far = pltpu.roll(near, 64, 1)
        even_group = lax.rem(me, 2) == 0
        twice = jnp.where(half == even_group, near, far)
        for t in range(4):
            kept = jnp.where(half == (t % 2 == 0), twice, nothing)
            sides = [kept, nothing] if t < 2 else [nothing, kept]
            weights[k * SPAN + t * 64 : k * SPAN + (t + 1) * 64, :] = jnp.concatenate(sides, axis=1).astype(jnp.bfloat16)

    def own_window(r, c):
        window(x_ref[r], r + HALO)
        return c

    lax.fori_loop(0, 2 * STEP + HALO, own_window, 0)
    pl.semaphore_wait(barrier, 5)

    def halo_copy(n):
        return pltpu.make_async_remote_copy(
            src_ref=x_ref.at[pl.ds(rows - HALO if n == 0 else 0, HALO)],
            dst_ref=halo.at[n],
            send_sem=halo_send.at[n],
            recv_sem=halo_recv.at[n],
            device_id={"lat": above if n == 0 else below},
            device_id_type=pl.DeviceIdType.MESH,
        )

    for n in range(2):
        halo_copy(n).start()

    def chunk_copy(step, d):
        return pltpu.make_async_remote_copy(
            src_ref=send.at[partners[d], pl.ds(step * 2, 2)],
            dst_ref=recv.at[me, pl.ds(step * 2, 2)],
            send_sem=send_sem.at[d, step],
            recv_sem=recv_sem.at[d, step],
            device_id={"lon": partners[d]},
            device_id_type=pl.DeviceIdType.MESH,
        )

    low = lax.broadcasted_iota(jnp.int32, (LINES, 128), 1) < 64

    def body(idx, c):
        step = lax.rem(idx + 1, steps)

        @pl.when(idx == steps - 2)
        def _():
            for n in range(2):
                halo_copy(n).wait()
                for r in range(HALO):
                    window(halo[n, r], r + n * (rows + HALO))

        for r in range(STEP):
            i = step * STEP + r
            for k0 in range(0, BASIS, 3):
                acc = None
                for s in range(SLOTS):
                    b = jnp.where(s < live_ref[i], band_ref[i * SLOTS + s], 8)
                    part = lax.dot_general(
                        bank[pl.ds(b * BASIS + k0, 3)].reshape(3 * LINES, SPAN),
                        field[i + HALO + off_ref[i * SLOTS + s]],
                        NT,
                        preferred_element_type=jnp.float32,
                    )
                    acc = part if acc is None else acc + part
                for k in range(3):
                    quad[r * LINES : (r + 1) * LINES, (k0 + k) * SPAN : (k0 + k + 1) * SPAN] = acc[k * LINES : (k + 1) * LINES].astype(jnp.bfloat16)
        for r in range(STEP):
            ahead = jnp.minimum((idx + 2) * STEP + HALO + r, rows - 1)
            window(x_ref[ahead], ahead + HALO)
        mixed = jnp.dot(quad[...], weights[...], preferred_element_type=jnp.float32)
        for p in range(STEP // 2):
            even = mixed[2 * p * LINES : (2 * p + 1) * LINES]
            odd = mixed[(2 * p + 1) * LINES : (2 * p + 2) * LINES]
            for h in range(2):
                e = even[:, h * 128 : (h + 1) * 128]
                o = odd[:, h * 128 : (h + 1) * 128]
                send[2 * h, step * 2 + p] = jnp.where(low, e, pltpu.roll(o, 64, 1)).astype(jnp.bfloat16)
                send[2 * h + 1, step * 2 + p] = jnp.where(low, pltpu.roll(e, 64, 1), o).astype(jnp.bfloat16)
        for d in range(3):
            chunk_copy(step, d).start()
        return c

    lax.fori_loop(0, steps, body, 0)

    def assemble(idx, c):
        step = lax.rem(idx + 1, steps)
        for d in range(3):
            chunk_copy(step, d).wait()
        recv[me, pl.ds(step * 2, 2)] = send[me, pl.ds(step * 2, 2)]
        for p in range(STEP // 2):
            pair = step * 2 + p
            for h in range(2):
                a = recv[2 * h, pair].astype(jnp.float32)
                b = recv[2 * h + 1, pair].astype(jnp.float32)
                out_ref[2 * pair, :, h * 128 : (h + 1) * 128] = jnp.where(low, a, pltpu.roll(b, 64, 1)).astype(jnp.bfloat16)[:TILE]
                out_ref[2 * pair + 1, :, h * 128 : (h + 1) * 128] = jnp.where(low, pltpu.roll(a, 64, 1), b).astype(jnp.bfloat16)[:TILE]
        return c

    lax.fori_loop(0, steps, assemble, 0)


def grouped_plan(band_field, offsets, live_counts, band_ids, tap_bank, mixing):
    rows = band_field.shape[0]
    steps = rows // STEP
    sm = pl.BlockSpec(memory_space=pltpu.SMEM)
    vm = pl.BlockSpec(memory_space=pltpu.VMEM)
    return pl.pallas_call(
        kernel,
        out_shape=jax.ShapeDtypeStruct((rows, TILE, 256), jnp.bfloat16),
        in_specs=[sm, sm, sm, vm, vm, vm],
        out_specs=vm,
        scratch_shapes=[
            pltpu.VMEM((81, LINES, SPAN), jnp.bfloat16),
            pltpu.VMEM((rows + 2 * HALO, SPAN, SPAN), jnp.bfloat16),
            pltpu.VMEM((2, HALO, 64, 360), jnp.bfloat16),
            pltpu.VMEM((BASIS * SPAN, SPAN), jnp.bfloat16),
            pltpu.VMEM((STEP * LINES, BASIS * SPAN), jnp.bfloat16),
            pltpu.VMEM((4, rows // 2, LINES, 128), jnp.bfloat16),
            pltpu.VMEM((4, rows // 2, LINES, 128), jnp.bfloat16),
            pltpu.SemaphoreType.DMA((3, steps)),
            pltpu.SemaphoreType.DMA((3, steps)),
            pltpu.SemaphoreType.DMA((2,)),
            pltpu.SemaphoreType.DMA((2,)),
        ],
        compiler_params=pltpu.CompilerParams(vmem_limit_bytes=48 * 2**20, collective_id=0, has_side_effects=True),
    )(offsets.reshape(-1), live_counts, band_ids.reshape(-1), band_field, tap_bank, mixing)


def solution(mesh):
    def on_device(*args):
        field = args[0]
        grouped = field.shape[1] == 64 and field.shape[2] == 4 * TILE and mesh.shape["lon"] == 4 and mesh.shape["lat"] > 1
        if grouped and field.shape[0] % STEP == 0 and field.shape[0] >= 4 * STEP:
            return grouped_plan(*args)
        return tiled_plan(*args)

    placed = (P(("ens", "lat"), "lon", None), P("lat", None), P("lat"), P("lat", None), P(), P())
    return jax.shard_map(
        on_device,
        mesh=mesh,
        in_specs=placed,
        out_specs=P(("ens", "lat"), "lon", None),
        check_vma=False,
    )
```

```python
import jax
import jax.numpy as jnp
from jax import lax
from jax.experimental import pallas as pl
from jax.experimental.pallas import tpu as pltpu
from jax.sharding import PartitionSpec as P

GROUPS = 4
BASIS = 9
REACH = 64
HALO = 3
SLOTS = 4


def extended_2(x, sides, width, wrap):
    for axis, dim in sides:
        size, length = (lax.axis_size(axis), x.shape[dim])
        up = [(i, (i + 1) % size) for i in range(size if wrap else size - 1)]
        down = [(j, i) for i, j in up]
        last = lax.slice_in_dim(x, length - width, length, axis=dim)
        first = lax.slice_in_dim(x, 0, width, axis=dim)
        before = lax.ppermute(last, axis, up)
        after = lax.ppermute(first, axis, down)
        x = jnp.concatenate([before, x, after], axis=dim)
    return x


def tiled_plan(band_field, offsets, live_counts, band_ids, tap_bank, mixing):
    tiles = lax.all_to_all(band_field, "lon", split_axis=2, concat_axis=1, tiled=True)
    widened = extended_2(tiles, (("lon", 2),), REACH, True)
    extended = extended_2(widened, (("lat", 0),), HALO, False)
    channels = extended.shape[1]
    span_cells = extended.shape[2]
    lon_cells = span_cells - 2 * REACH
    group_width = channels // GROUPS
    mixing_split = mixing.reshape(BASIS, group_width, GROUPS, group_width)
    distance = lax.broadcasted_iota(jnp.int32, (span_cells, lon_cells), 0) - lax.broadcasted_iota(
        jnp.int32, (span_cells, lon_cells), 1
    )
    inside = (distance >= 0) & (distance < 2 * REACH)
    picked = jnp.take(tap_bank, jnp.clip(distance, 0, 2 * REACH - 1), axis=2)
    toeplitz = jnp.where(inside, picked, jnp.zeros((), tap_bank.dtype))

    def slot_term(row_index, offset, band_index):
        source = lax.dynamic_index_in_dim(extended, row_index + HALO + offset, 0, keepdims=False)
        matrix = lax.dynamic_index_in_dim(toeplitz, band_index, 1, keepdims=False)
        return jnp.einsum("cj,kjl->kcl", source, matrix, preferred_element_type=jnp.float32)

    def one_row(packed):
        row_index, offset_row, live_count, band_row = packed
        summed = jnp.zeros((BASIS, channels, lon_cells), jnp.float32)
        for slot_index in range(SLOTS):
            live_mask = (slot_index < live_count).astype(jnp.float32)
            summed = summed + live_mask * slot_term(
                row_index, offset_row[slot_index], band_row[slot_index]
            )
        quadrature = summed.astype(jnp.bfloat16).reshape(BASIS, GROUPS, group_width, lon_cells)
        mixed_rows = jnp.einsum(
            "kcgo,kgcl->lgo", mixing_split, quadrature, preferred_element_type=jnp.float32
        )
        return mixed_rows.reshape(lon_cells, channels).astype(jnp.bfloat16)

    local_rows = jnp.arange(offsets.shape[0], dtype=jnp.int32)
    return lax.map(one_row, (local_rows, offsets, live_counts, band_ids))


NT = (((1,), (1,)), ((), ()))
STEP = 4
TILE = 90
SPAN = 256
LINES = 96


def kernel(off_in, live_in, band_in, x_in, taps_in, mix_in, out_hbm, off_ref, live_ref, band_ref, x_ref, taps_ref, mix_ref, load_sem, out_ref, store_sem, bank, field, halo, weights, quad, send, recv, send_sem, recv_sem, halo_send, halo_recv):
    me = lax.axis_index("lon")
    lat = lax.axis_index("lat")
    n_lat = lax.axis_size("lat")
    rows = x_ref.shape[0]
    steps = rows // STEP
    above, below = lax.rem(lat + 1, n_lat), lax.rem(lat + n_lat - 1, n_lat)
    partners = [lax.rem(me + d, 4) for d in range(1, 4)]
    sources = [lax.rem(me + 4 - d, 4) for d in range(1, 4)]

    pairs = [(taps_in, taps_ref), (mix_in, mix_ref), (x_in, x_ref), (off_in, off_ref), (live_in, live_ref), (band_in, band_ref)]
    loads = [pltpu.make_async_copy(a, b, load_sem.at[n]) for n, (a, b) in enumerate(pairs)]
    for load in loads:
        load.start()
    barrier = pltpu.get_barrier_semaphore()
    for p in partners:
        pl.semaphore_signal(barrier, inc=1, device_id={"lon": p}, device_id_type=pl.DeviceIdType.MESH)
    for q in (above, below):
        pl.semaphore_signal(barrier, inc=1, device_id={"lat": q}, device_id_type=pl.DeviceIdType.MESH)

    def window(x, slot):
        for t in range(4):
            s = (TILE * t - REACH) % 360
            if s + SPAN > 360:
                piece = jnp.concatenate([x[:, s:], x[:, : SPAN - 360 + s]], axis=1)
            else:
                piece = x[:, s : s + SPAN]
            field[slot, t * 64 : (t + 1) * 64, :] = piece

    def bank_blocks(k, c):
        taps = taps_ref[k].astype(jnp.float32)
        taps = jnp.concatenate([taps, jnp.zeros_like(taps)], axis=1)
        for b in range(8):
            line = jnp.broadcast_to(taps[b : b + 1], (16, SPAN))
            base = pltpu.roll(line, 0, 1, stride=1, stride_axis=0).astype(jnp.bfloat16)
            bank[b * BASIS + k, 0:16] = base
            for j in range(1, LINES // 16):
                bank[b * BASIS + k, 16 * j : 16 * (j + 1)] = jnp.concatenate([base[:, SPAN - 16 * j :], base[:, : SPAN - 16 * j]], axis=1)
        return c

    loads[0].wait()
    lax.fori_loop(0, BASIS, bank_blocks, 0)
    bank[72:81] = jnp.zeros((9, LINES, SPAN), jnp.bfloat16)
    half = lax.broadcasted_iota(jnp.int32, (64, 128), 1) < 64
    nothing = jnp.zeros((64, 128), jnp.float32)
    loads[1].wait()
    for k in range(BASIS):
        mix = mix_ref[k].astype(jnp.float32)
        near = jnp.where(me < 2, mix[:, :128], mix[:, 128:])
        far = pltpu.roll(near, 64, 1)
        even_group = lax.rem(me, 2) == 0
        twice = jnp.where(half == even_group, near, far)
        for t in range(4):
            kept = jnp.where(half == (t % 2 == 0), twice, nothing)
            sides = [kept, nothing] if t < 2 else [nothing, kept]
            weights[k * SPAN + t * 64 : k * SPAN + (t + 1) * 64, :] = jnp.concatenate(sides, axis=1).astype(jnp.bfloat16)

    def own_window(r, c):
        window(x_ref[r], r + HALO)
        return c

    for load in loads[2:]:
        load.wait()
    lax.fori_loop(0, 2 * STEP + HALO, own_window, 0)
    pl.semaphore_wait(barrier, 5)

    def halo_copy(n):
        return pltpu.make_async_remote_copy(
            src_ref=x_ref.at[pl.ds(rows - HALO if n == 0 else 0, HALO)],
            dst_ref=halo.at[n],
            send_sem=halo_send.at[n],
            recv_sem=halo_recv.at[n],
            device_id={"lat": above if n == 0 else below},
            device_id_type=pl.DeviceIdType.MESH,
        )

    for n in range(2):
        halo_copy(n).start()

    def chunk_copy(step, d):
        return pltpu.make_async_remote_copy(
            src_ref=send.at[partners[d], pl.ds(step * 2, 2)],
            dst_ref=recv.at[me, pl.ds(step * 2, 2)],
            send_sem=send_sem.at[d, step],
            recv_sem=recv_sem.at[d, step],
            device_id={"lon": partners[d]},
            device_id_type=pl.DeviceIdType.MESH,
        )

    low = lax.broadcasted_iota(jnp.int32, (LINES, 128), 1) < 64

    def body(idx, c):
        step = lax.rem(idx + 1, steps)

        @pl.when(idx == steps - 2)
        def _():
            for n in range(2):
                halo_copy(n).wait()
                for r in range(HALO):
                    window(halo[n, r], r + n * (rows + HALO))

        for r in range(STEP):
            i = step * STEP + r
            for k0 in range(0, BASIS, 3):
                acc = None
                for s in range(SLOTS):
                    b = jnp.where(s < live_ref[i], band_ref[s, i], 8)
                    part = lax.dot_general(
                        bank[pl.ds(b * BASIS + k0, 3)].reshape(3 * LINES, SPAN),
                        field[i + HALO + off_ref[s, i]],
                        NT,
                        preferred_element_type=jnp.float32,
                    )
                    acc = part if acc is None else acc + part
                for k in range(3):
                    quad[r * LINES : (r + 1) * LINES, (k0 + k) * SPAN : (k0 + k + 1) * SPAN] = acc[k * LINES : (k + 1) * LINES].astype(jnp.bfloat16)
        for r in range(STEP):
            ahead = jnp.minimum((idx + 2) * STEP + HALO + r, rows - 1)
            window(x_ref[ahead], ahead + HALO)
        mixed = jnp.dot(quad[...], weights[...], preferred_element_type=jnp.float32)
        for p in range(STEP // 2):
            even = mixed[2 * p * LINES : (2 * p + 1) * LINES]
            odd = mixed[(2 * p + 1) * LINES : (2 * p + 2) * LINES]
            for h in range(2):
                e = even[:, h * 128 : (h + 1) * 128]
                o = odd[:, h * 128 : (h + 1) * 128]
                send[2 * h, step * 2 + p] = jnp.where(low, e, pltpu.roll(o, 64, 1)).astype(jnp.bfloat16)
                send[2 * h + 1, step * 2 + p] = jnp.where(low, pltpu.roll(e, 64, 1), o).astype(jnp.bfloat16)
        for d in range(3):
            chunk_copy(step, d).start()
        return c

    lax.fori_loop(0, steps, body, 0)

    def store(step):
        cells = pl.ds(step * STEP, STEP)
        return pltpu.make_async_copy(out_ref.at[cells], out_hbm.at[cells], store_sem.at[step])

    def assemble(idx, c):
        step = lax.rem(idx + 1, steps)
        for d in range(3):
            chunk_copy(step, d).wait()
        recv[me, pl.ds(step * 2, 2)] = send[me, pl.ds(step * 2, 2)]
        for p in range(STEP // 2):
            pair = step * 2 + p
            for h in range(2):
                a = recv[2 * h, pair].astype(jnp.float32)
                b = recv[2 * h + 1, pair].astype(jnp.float32)
                out_ref[2 * pair, :, h * 128 : (h + 1) * 128] = jnp.where(low, a, pltpu.roll(b, 64, 1)).astype(jnp.bfloat16)[:TILE]
                out_ref[2 * pair + 1, :, h * 128 : (h + 1) * 128] = jnp.where(low, pltpu.roll(a, 64, 1), b).astype(jnp.bfloat16)[:TILE]
        store(step).start()
        return c

    def finish(step, c):
        store(step).wait()
        return c

    lax.fori_loop(0, steps, assemble, 0)
    lax.fori_loop(0, steps, finish, 0)


def grouped_plan(band_field, offsets, live_counts, band_ids, tap_bank, mixing):
    rows = band_field.shape[0]
    steps = rows // STEP
    hbm = pl.BlockSpec(memory_space=pltpu.HBM)
    return pl.pallas_call(
        kernel,
        out_shape=jax.ShapeDtypeStruct((rows, TILE, 256), jnp.bfloat16),
        in_specs=[hbm] * 6,
        out_specs=hbm,
        scratch_shapes=[
            pltpu.SMEM((SLOTS, rows), jnp.int32),
            pltpu.SMEM((rows,), jnp.int32),
            pltpu.SMEM((SLOTS, rows), jnp.int32),
            pltpu.VMEM(band_field.shape, jnp.bfloat16),
            pltpu.VMEM(tap_bank.shape, jnp.bfloat16),
            pltpu.VMEM(mixing.shape, jnp.bfloat16),
            pltpu.SemaphoreType.DMA((6,)),
            pltpu.VMEM((rows, TILE, 256), jnp.bfloat16),
            pltpu.SemaphoreType.DMA((steps,)),
            pltpu.VMEM((81, LINES, SPAN), jnp.bfloat16),
            pltpu.VMEM((rows + 2 * HALO, SPAN, SPAN), jnp.bfloat16),
            pltpu.VMEM((2, HALO, 64, 360), jnp.bfloat16),
            pltpu.VMEM((BASIS * SPAN, SPAN), jnp.bfloat16),
            pltpu.VMEM((STEP * LINES, BASIS * SPAN), jnp.bfloat16),
            pltpu.VMEM((4, rows // 2, LINES, 128), jnp.bfloat16),
            pltpu.VMEM((4, rows // 2, LINES, 128), jnp.bfloat16),
            pltpu.SemaphoreType.DMA((3, steps)),
            pltpu.SemaphoreType.DMA((3, steps)),
            pltpu.SemaphoreType.DMA((2,)),
            pltpu.SemaphoreType.DMA((2,)),
        ],
        compiler_params=pltpu.CompilerParams(vmem_limit_bytes=63 * 2**20, collective_id=0, has_side_effects=True),
    )(offsets.T, live_counts, band_ids.T, band_field, tap_bank, mixing)


def solution(mesh):
    def on_device(*args):
        field = args[0]
        grouped = field.shape[1] == 64 and field.shape[2] == 4 * TILE and mesh.shape["lon"] == 4 and mesh.shape["lat"] > 1
        if grouped and field.shape[0] % STEP == 0 and field.shape[0] >= 4 * STEP:
            return grouped_plan(*args)
        return tiled_plan(*args)

    placed = (P(("ens", "lat"), "lon", None), P("lat", None), P("lat"), P("lat", None), P(), P())
    return jax.shard_map(
        on_device,
        mesh=mesh,
        in_specs=placed,
        out_specs=P(("ens", "lat"), "lon", None),
        check_vma=False,
    )
```
